128 devices in a mesh: section: 2 (over core), fsdp: 4 (over z), ctx: 16 (over y, x).
Axes of the slice: x: 4, y: 4, z: 4, core: 2. Of those that a mesh axis runs over, the one named last changes fastest.
Arguments:
- layer_input: bfloat16 [2, 4, 2048, 1536], P(None, 'fsdp', 'ctx'), may hold values from -6 to 6
- output_grad: bfloat16 [2, 4, 2048, 1536], P(None, 'fsdp', 'ctx'), may hold values from -6 to 6
- seq_lengths: int32 [2, 4], P(None, 'fsdp'), may hold values from 1024 to 2048, as said below
- norm_gain: bfloat16 [2, 1536], P('section', ('fsdp', 'ctx')), may hold values from 0.5 to 1.5
- in_proj: bfloat16 [2, 1536, 6448], P('section', ('fsdp', 'ctx')), may hold values from -0.15625 to 0.15625
- conv_weight: bfloat16 [2, 4, 3328], P('section', None, ('fsdp', 'ctx')), may hold values from -3 to 3
- conv_bias: bfloat16 [2, 3328], P('section', ('fsdp', 'ctx')), may hold values from -3 to 3
- gate_gain: bfloat16 [2, 3072], P('section', ('fsdp', 'ctx')), may hold values from 0.5 to 1.5
- out_proj: bfloat16 [2, 3072, 1536], P('section', ('fsdp', 'ctx')), may hold values from -0.109375 to 0.109375
- decay_log: float32 [2, 48], P('section'), may hold values from -6 to 1
- skip_gain: float32 [2, 48], P('section'), may hold values from 0.5 to 2
- step_bias: float32 [2, 48], P('section'), may hold values from -2 to 0
Outputs:
- activations: bfloat16 [2, 2, 4, 2048, 1536], P('section', None, 'fsdp', 'ctx')
- input_grad: float32 [2, 2, 4, 2048, 1536], P('section', None, 'fsdp', 'ctx')
- grad_norm_gain: float32 [2, 1536], P('section', ('fsdp', 'ctx'))
- grad_in_proj: float32 [2, 1536, 6448], P('section', ('fsdp', 'ctx'))
- grad_conv_weight: float32 [2, 4, 3328], P('section', None, ('fsdp', 'ctx'))
- grad_conv_bias: float32 [2, 3328], P('section', ('fsdp', 'ctx'))
- grad_gate_gain: float32 [2, 3072], P('section', ('fsdp', 'ctx'))
- grad_out_proj: float32 [2, 3072, 1536], P('section', ('fsdp', 'ctx'))
- grad_decay_log: float32 [2, 48], P('section')
- grad_skip_gain: float32 [2, 48], P('section')
- grad_step_bias: float32 [2, 48], P('section')
The draws below stay inside these ranges and needn't reach their ends.
Inputs may be any that keep to these rules, and one draw needn't show every extreme that they name: `seq_lengths`: in every sequence slot of fsdp, one of the two micro-batches holds a sequence of exactly 2048 positions; the others are at least 1024; positions beyond a length are padding.
All inputs are finite; a program needn't handle non-finite values.
Results may differ from the reference program's by a relative error of at most 0.017.
The reference program's roundings to bfloat16 on the way (of `normed` and `normed_two`) count: a program that leaves them out, or rounds other values in their place, can miss the bound.
Values may be sent and summed in bfloat16 or wider, within the bound.
A program may use at most 320 MiB of HBM per device.

```python
import jax
import jax.numpy as jnp
from jax import lax

D = 1536
DI = 3072
H = 48
P_SIZE = 64
N = 128
K = 4
TOK_MB = 128
MICRO = 2
CONV = 3328
E = 6448
STREAM = 2048
SEQS = 4
SHORTEST = 1024


def draw_seq_lengths(key, part):
    key = jax.random.fold_in(key, 11)
    first_key, second_key = jax.random.split(key)
    drawn_lengths = jax.random.randint(first_key, (MICRO, SEQS), SHORTEST, STREAM + 1)
    full_at = jax.random.randint(second_key, (SEQS,), 0, MICRO)
    micro_ids = jnp.arange(MICRO)[:, None]
    return jnp.where(micro_ids == full_at[None, :], STREAM, drawn_lengths).astype(jnp.int32)


def level_of(stream_key, shape, cuts, smallest, top_value):
    level, own = 1.0, jax.random.fold_in(stream_key, 6)
    for axis_at, blocks in cuts:
        steps = jnp.exp(jax.random.uniform(jax.random.fold_in(own, axis_at), (blocks,), jnp.float32, smallest / len(cuts), top_value / len(cuts)))
        level = level * jnp.repeat(steps, shape[axis_at] // blocks).reshape([-1 if axis == axis_at else 1 for axis in range(len(shape))])
    return level


def gaussian(key, shape, spread, most, cuts=(), kind=jnp.bfloat16):
    values = jax.random.normal(key, shape, jnp.float32) * spread
    if len(cuts) > 0:
        values = level_of(key, shape, cuts, -0.22, 0.18) * values
    return jnp.clip(values, min=-most, max=most).astype(kind)


def setup_inputs(seed: int = 0) -> dict:
    keys = jax.random.split(jax.random.key(seed), 13)
    return {
        "layer_input": gaussian(keys[0], (MICRO, SEQS, STREAM, D), 1.0, 6.0, ((1, 4), (2, 16))),
        "output_grad": gaussian(keys[1], (MICRO, SEQS, STREAM, D), 1.0, 6.0, ((1, 4), (2, 16))),
        "seq_lengths": draw_seq_lengths(jax.random.fold_in(keys[12], 71), 0),
        "norm_gain": jnp.clip(1.0 + 0.1 * jax.random.normal(keys[3], (2, D), jnp.float32), 0.5, 1.5).astype(jnp.bfloat16),
        "in_proj": gaussian(keys[4], (2, D, E), D ** -0.5, 0.15625, ((0, 2), (1, 64))),
        "conv_weight": gaussian(keys[5], (2, K, CONV), K ** -0.5, 3.0, ((0, 2), (2, 64))),
        "conv_bias": gaussian(keys[6], (2, CONV), 0.5, 3.0, ((0, 2), (1, 64))),
        "gate_gain": jnp.clip(1.0 + 0.1 * jax.random.normal(keys[7], (2, DI), jnp.float32), 0.5, 1.5).astype(jnp.bfloat16),
        "out_proj": gaussian(keys[8], (2, DI, D), DI ** -0.5, 0.109375, ((0, 2), (1, 64))),
        "decay_log": jnp.clip(-6.0 + 7.0 * jax.random.uniform(keys[9], (2, H), jnp.float32) ** level_of(keys[9], (2, H), ((0, 2),), -0.2, 0.2), -6.0, 1.0),
        "skip_gain": jnp.clip(0.5 + 1.5 * jax.random.uniform(keys[10], (2, H), jnp.float32) ** level_of(keys[10], (2, H), ((0, 2),), -0.2, 0.2), 0.5, 2.0),
        "step_bias": jnp.clip(-2.0 + 2.0 * jax.random.uniform(keys[11], (2, H), jnp.float32) ** level_of(keys[11], (2, H), ((0, 2),), -0.2, 0.2), -2.0, 0.0),
    }


EPSILON = 1e-05
HIGHEST = lax.Precision.HIGHEST

@jax.custom_vjp
def low(v):
    return lax.optimization_barrier(v.astype(jnp.bfloat16)).astype(jnp.float32)

@jax.custom_vjp
def low_back(v):
    return v

def low_keep(v):
    return (low(v), None)

def low_pass(kept, grad):
    return (grad,)

def back_keep(v):
    return (v, None)

def back_low(kept, grad):
    return (low(grad),)
low.defvjp(low_keep, low_pass)
low_back.defvjp(back_keep, back_low)

def rms_scale(values, gain):
    return values * lax.rsqrt(lax.optimization_barrier(jnp.mean(values * values, axis=-1, keepdims=True)) + EPSILON) * gain

def span_step(state_in, pieces, decay_log, skip_gain):
    values, input_map, output_map, step_size = pieces
    length = values.shape[0]
    log_decay = jnp.cumsum(step_size * (-jnp.exp(decay_log))[None, :], axis=0)
    ordinal = jnp.arange(length)
    causal = (ordinal[:, None] >= ordinal[None, :])[:, :, None]
    decay_gap = log_decay[:, None, :] - log_decay[None, :, :]
    decay_mat = jnp.where(causal, jnp.exp(jnp.where(causal, decay_gap, 0.0)), 0.0)
    intersection = jnp.dot(output_map, input_map.T, precision=HIGHEST)
    weights = decay_mat * intersection[:, :, None] * step_size[None, :, :]
    within = jnp.einsum('tsh,shp->thp', weights, values, precision=HIGHEST)
    carried = jnp.exp(log_decay)[:, :, None] * jnp.einsum('tn,hpn->thp', output_map, state_in, precision=HIGHEST)
    result = within + carried + skip_gain[None, :, None] * values
    tail_weight = jnp.exp(log_decay[-1][None, :] - log_decay) * step_size
    local_state = jnp.einsum('shp,sn->hpn', tail_weight[:, :, None] * values, input_map, precision=HIGHEST)
    new_state = jnp.exp(log_decay[-1])[:, None, None] * state_in + local_state
    return (new_state, result)

def mamba_layer(series, valid_rows, params):
    norm_gain, in_proj, conv_weight, conv_bias, gate_gain, out_proj, decay_log, skip_gain, step_bias = params
    length = series.shape[0]
    normed = low(rms_scale(series, norm_gain))
    projected = low_back(jnp.dot(normed, in_proj, precision=HIGHEST))
    conv_in = projected[:, DI:DI + CONV]
    padded = jnp.concatenate([jnp.zeros((K - 1, CONV), jnp.float32), conv_in], axis=0)
    summed = conv_bias[None, :] + jnp.zeros_like(conv_in)
    for offset in range(K):
        summed = summed + conv_weight[offset][None, :] * padded[offset:offset + length]
    activated = jax.nn.silu(summed)
    step_size = jax.nn.softplus(projected[:, DI + CONV:] + step_bias[None, :])
    blocks = length // TOK_MB
    pieces = (activated[:, :DI].reshape(blocks, TOK_MB, H, P_SIZE), activated[:, DI:DI + N].reshape(blocks, TOK_MB, N), activated[:, DI + N:].reshape(blocks, TOK_MB, N), step_size.reshape(blocks, TOK_MB, H))

    def advance(state_in, piece):
        return span_step(state_in, piece, decay_log, skip_gain)
    final_state, outputs = lax.scan(jax.checkpoint(advance), jnp.zeros((H, P_SIZE, N), jnp.float32), pieces)
    mixed_out = outputs.reshape(length, DI)
    gated_out = mixed_out * jax.nn.silu(projected[:, :DI])
    normed_two = low(rms_scale(gated_out, gate_gain))
    branch = low_back(jnp.dot(normed_two, out_proj, precision=HIGHEST))
    return valid_rows[:, None] * (series + branch)

def reference(layer_input, output_grad, seq_lengths, norm_gain, in_proj, conv_weight, conv_bias, gate_gain, out_proj, decay_log, skip_gain, step_bias):
    positions = jnp.arange(STREAM).astype(jnp.int32)
    valid_rows = (positions[None, None, :] < seq_lengths[:, :, None]).astype(jnp.float32).reshape(MICRO * SEQS, STREAM)
    inputs = layer_input.astype(jnp.float32).reshape(MICRO * SEQS, STREAM, D)
    params = (norm_gain.astype(jnp.float32), in_proj.astype(jnp.float32), conv_weight.astype(jnp.float32), conv_bias.astype(jnp.float32), gate_gain.astype(jnp.float32), out_proj.astype(jnp.float32), decay_log.astype(jnp.float32), skip_gain.astype(jnp.float32), step_bias.astype(jnp.float32))
    runner = jax.checkpoint(mamba_layer)

    def forward(inputs, params, nudge_term):
        params_one = tuple((weight_item[0] for weight_item in params))
        params_two = tuple((weight_item[1] for weight_item in params))

        def section_one(pair_rows):
            return runner(pair_rows[0], pair_rows[1], params_one)

        def section_two(pair_rows):
            return runner(pair_rows[0], pair_rows[1], params_two)
        first_out = lax.map(section_one, (inputs, valid_rows))
        handed = low_back(low(first_out)) + nudge_term
        second_out = lax.map(section_two, (handed, valid_rows))
        return (first_out, second_out)
    nudge_term = jnp.zeros_like(inputs)
    (first_out, second_out), pullback = jax.vjp(forward, inputs, params, nudge_term)
    cotangent = output_grad.astype(jnp.float32).reshape(MICRO * SEQS, STREAM, D)
    grad_input, grad_params, grad_nudge = pullback((jnp.zeros_like(first_out), cotangent))
    activations = jnp.stack([first_out, second_out]).reshape(2, MICRO, SEQS, STREAM, D).astype(jnp.bfloat16)
    input_grad = jnp.stack([grad_input, grad_nudge]).reshape(2, MICRO, SEQS, STREAM, D)
    return (activations, input_grad, grad_params[0], grad_params[1], grad_params[2], grad_params[3], grad_params[4], grad_params[5], grad_params[6], grad_params[7], grad_params[8])
```

```python
import functools

import jax
import jax.numpy as jnp
from jax import lax
from jax.experimental import pallas as pl
from jax.experimental.pallas import tpu as pltpu
from jax.sharding import PartitionSpec as P

D = 1536
DI = 3072
H = 48
PS = 64
N = 128
K = 4
CONV = 3328
E = 6448
TP = 4
T = 128
ROWS = 512
HALO = 16
EXT = ROWS + HALO
CHUNKS = ROWS // T
HL = H // TP
XW = HL * PS
UW = XW + 2 * N
EW = XW + UW + 128
RAW = XW + UW
EPS = 1e-05
f32 = jnp.float32
bf16 = jnp.bfloat16
ACC = lax.Precision.HIGH
FULL = lax.Precision.HIGHEST
VMEM_LIMIT = 56 * 1024 * 1024


def dot(a, b, precision=None):
    return lax.dot_general(a, b, (((1,), (0,)), ((), ())), precision=precision, preferred_element_type=f32)


def dot_nt(a, b, precision=None):
    return lax.dot_general(a, b, (((1,), (1,)), ((), ())), precision=precision, preferred_element_type=f32)


def dot_tn(a, b, precision=None):
    return lax.dot_general(a, b, (((0,), (0,)), ((), ())), precision=precision, preferred_element_type=f32)


def iota(shape, axis):
    return lax.broadcasted_iota(jnp.int32, shape, axis)


def expander():
    return jnp.where(iota((128, XW), 1) // PS == iota((128, XW), 0), 1.0, 0.0).astype(f32)


def sigmoid(v):
    return 1.0 / (1.0 + jnp.exp(-v))


def softplus(v):
    return jnp.maximum(v, 0.0) + jnp.log1p(jnp.exp(-jnp.abs(v)))


def tri_lower():
    return iota((T, T), 0) >= iota((T, T), 1)


def pair_mask():
    return iota((T, 128), 1) < PS


MESH = pl.DeviceIdType.MESH
ANY = pl.ANY
VMEM = pltpu.VMEM


def remote(src, dst, send, recv, where):
    return pltpu.make_async_remote_copy(
        src_ref=src, dst_ref=dst, send_sem=send, recv_sem=recv, device_id=where, device_id_type=MESH
    )


def greet(peers):
    barrier = pltpu.get_barrier_semaphore()
    for peer in peers:
        pl.semaphore_signal(barrier, inc=1, device_id=peer, device_id_type=MESH)
    return barrier


def around(axis):
    me = lax.axis_index(axis)
    return me, lax.rem(me + 1, TP), lax.rem(me + 3, TP), lax.rem(me + 2, TP)


class Ring:
    def __init__(self, axis, view, own, sends, recvs, arrived=None):
        self.axis, self.view, self.own, self.sends, self.recvs = axis, view, own, sends, recvs
        self.arrived = arrived or (lambda block, half, slot: None)
        self.me, self.right, self.left, self.across = around(axis)

    def copy(self, src, block, half, slot, to):
        return remote(src, self.view(block, half), self.sends.at[slot], self.recvs.at[slot], {self.axis: to})

    def prepare(self):
        me = self.me
        self.copies = [
            self.copy(self.own(0), me, 0, 0, self.right),
            self.copy(self.own(1), me, 1, 1, self.left),
            self.copy(self.own(1), me, 1, 2, self.right),
            self.copy(self.own(0), me, 0, 3, self.left),
        ]

    def start(self):
        self.prepare()
        for c in self.copies:
            c.start()

    def forward(self):
        self.copies[0].wait_recv()
        on = self.copy(self.view(self.left, 0), self.left, 0, 4, self.right)
        on.start()
        self.arrived(self.left, 0, 0)
        self.copies[1].wait_recv()
        back = self.copy(self.view(self.right, 1), self.right, 1, 5, self.left)
        back.start()
        self.arrived(self.right, 1, 1)
        self.copies = self.copies[:4] + [on, back]

    def rebuild(self):
        self.copies = self.copies[:4] + [
            self.copy(self.view(self.left, 0), self.left, 0, 4, self.right),
            self.copy(self.view(self.right, 1), self.right, 1, 5, self.left),
        ]

    def finish(self):
        for slot, (block, half) in ((2, (self.left, 1)), (3, (self.right, 0)), (4, (self.across, 0)), (5, (self.across, 1))):
            self.copies[slot].wait_recv()
            self.arrived(block, half, slot)
        for c in self.copies:
            c.wait_send()


def comm_call(body, outs, inputs, scratch, collective_id, sent):
    return pl.pallas_call(
        body,
        out_shape=[jax.ShapeDtypeStruct(s, d) for s, d, _ in outs],
        in_specs=[pl.BlockSpec(memory_space=m) for m in inputs],
        out_specs=[pl.BlockSpec(memory_space=m) for _, _, m in outs],
        scratch_shapes=scratch,
        cost_estimate=pl.CostEstimate(flops=0, bytes_accessed=sent, transcendentals=0),
        compiler_params=pltpu.CompilerParams(
            collective_id=collective_id, has_side_effects=True, vmem_limit_bytes=VMEM_LIMIT
        ),
    )


def sems(*shape):
    return pltpu.SemaphoreType.DMA(shape)


def add_tiles(target, *terms):
    leads = [()] if len(target.shape) == 2 else [(i,) for i in range(target.shape[0])]

    def tile(i, carry):
        at = pl.ds(pl.multiple_of(i * 16, 16), 16)
        for lead in leads:
            total = terms[0][lead + (at,)].astype(f32)
            for term in terms[1:]:
                total = total + term[lead + (at,)].astype(f32)
            target[lead + (at,)] = total.astype(target.dtype)
        return carry

    lax.fori_loop(0, target.shape[-2] // 16, tile, 0)


class RingSum:
    def __init__(self, axis, view, landed, relay, sends, recvs):
        self.axis, self.view, self.landed, self.relay, self.sends, self.recvs = axis, view, landed, relay, sends, recvs
        self.me, self.right, self.left, self.across = around(axis)

    def push(self, src, slot, to):
        half = slot % 2
        return remote(src, self.landed[half].at[slot // 2], self.sends.at[slot], self.recvs.at[slot], {self.axis: to})

    def prepare(self):
        self.copies = [
            self.push(self.view(self.across, 0), 0, self.right),
            self.push(self.view(self.across, 1), 1, self.left),
            self.push(self.view(self.left, 0), 2, self.left),
            self.push(self.view(self.right, 1), 3, self.right),
        ]

    def start(self):
        self.prepare()
        for c in self.copies:
            c.start()

    def forward(self):
        for half, block, to in ((0, self.right, self.right), (1, self.left, self.left)):
            self.copies[half].wait_recv()
            add_tiles(self.relay[half], self.landed[half].at[0], self.view(block, half))
            on = self.push(self.relay[half], 4 + half, to)
            on.start()
            self.copies.append(on)

    def rebuild(self):
        self.copies = self.copies[:4] + [
            self.push(self.relay[0], 4, self.right), self.push(self.relay[1], 5, self.left)
        ]

    def finish(self, target):
        for half in range(2):
            self.copies[2 + half].wait_recv()
            self.copies[4 + half].wait_recv()
            add_tiles(target(half), self.landed[half].at[1], self.landed[half].at[2], self.view(self.me, half))
        for c in self.copies:
            c.wait_send()


HALF = T // 2


def half_rows(start, block, half):
    return pl.ds(pl.multiple_of(start + block * T + half * HALF, 16), HALF)


def givers():
    x = lax.axis_index("x")
    y = lax.axis_index("y")
    return jnp.logical_and(x == TP - 1, y < TP - 1), y > 0


def next_rows(i):
    return {"y": lax.rem(lax.axis_index("y") + 1, TP), "x": i}


def rows_before():
    return {"y": lax.rem(lax.axis_index("y") + 3, TP), "x": TP - 1}


def greet_rows(barrier):
    @pl.when(lax.axis_index("y") > 0)
    def _():
        pl.semaphore_signal(barrier, inc=1, device_id=rows_before(), device_id_type=MESH)


class RowGather:
    def __init__(self, src, out, halo, sends, recvs, local, halo_sends=None, halo_recv=None, zeros=None):
        first = HALO if halo else 0
        x = lax.axis_index("x")
        self.ring = Ring(
            "x", lambda i, h: out.at[half_rows(first, i, h)], lambda h: src.at[pl.ds(h * HALF, HALF)], sends, recvs
        )
        self.own = pltpu.make_async_copy(src, out.at[pl.ds(pl.multiple_of(first + x * T, 16), T)], local.at[0])
        self.halo = halo
        if halo:
            self.blank = pltpu.make_async_copy(zeros, out.at[pl.ds(0, HALO)], local.at[1])
            self.gifts = [
                remote(
                    src.at[pl.ds(T - HALO, HALO)], out.at[pl.ds(0, HALO)], halo_sends.at[i], halo_recv.at[0], next_rows(i)
                )
                for i in range(TP)
            ]

    def start(self):
        self.own.start()
        self.ring.start()
        if self.halo:
            gives, has = givers()

            @pl.when(jnp.logical_not(has))
            def _():
                self.blank.start()

            @pl.when(gives)
            def _():
                for gift in self.gifts:
                    gift.start()

    def forward(self):
        self.ring.forward()

    def finish(self):
        self.ring.finish()
        self.own.wait()
        if self.halo:
            gives, has = givers()

            @pl.when(gives)
            def _():
                for gift in self.gifts:
                    gift.wait_send()

            @pl.when(has)
            def _():
                self.gifts[0].wait_recv()

            @pl.when(jnp.logical_not(has))
            def _():
                self.blank.wait()


class RowSum:
    def __init__(self, part, halo, landed, relay, sends, recvs, edges=None, edge_send=None, edge_recvs=None):
        first = HALO if halo else 0
        x = lax.axis_index("x")
        self.ring = RingSum(
            "x", lambda i, h: part.at[half_rows(first, i, h)], (landed.at[0], landed.at[1]), (relay.at[0], relay.at[1]),
            sends, recvs,
        )
        self.halo, self.edges = halo, edges
        if halo:
            self.from_next = [
                remote(part.at[pl.ds(0, HALO)], edges.at[i], edge_send.at[0], edge_recvs.at[i], rows_before())
                for i in range(TP)
            ]
            self.edge = remote(part.at[pl.ds(0, HALO)], edges.at[x], edge_send.at[0], edge_recvs.at[x], rows_before())

    def start(self):
        self.ring.start()
        if self.halo:

            @pl.when(givers()[1])
            def _():
                self.edge.start()

    def forward(self):
        self.ring.forward()

    def finish(self, out):
        self.ring.finish(lambda half: out.at[pl.ds(half * HALF, HALF)])
        if self.halo:
            gives, has = givers()

            @pl.when(gives)
            def _():
                added = jnp.zeros((HALO, D), f32)
                for i in range(TP):
                    self.from_next[i].wait_recv()
                    added = added + self.edges[i].astype(f32)
                out[T - HALO : T, :] += added

            @pl.when(has)
            def _():
                self.edge.wait_send()


def greet_edges(barrier):
    @pl.when(givers()[0])
    def _():
        for i in range(TP):
            pl.semaphore_signal(barrier, inc=1, device_id=next_rows(i), device_id_type=MESH)


def wait_counts(barrier, base, *more):
    if not more:
        pl.semaphore_wait(barrier, base)
        return
    (condition, count), rest = more[0], more[1:]

    @pl.when(condition)
    def _():
        wait_counts(barrier, base + count, *rest)

    @pl.when(jnp.logical_not(condition))
    def _():
        wait_counts(barrier, base, *rest)


def row_scale(values):
    return lax.rsqrt(jnp.mean(values * values, axis=-1, keepdims=True) + EPS)


SPLIT = 1024
OUT_SPLIT = 768


def first_two(half):
    return slice(0, 2) if half == 0 else slice(2, 4)


def half_piece(half):
    return pl.ds(48 * half, 48)


def thirds(half):
    return pl.ds(32, 16) if half else pl.ds(0, 32)


class WeightParts:
    def __init__(self, layer):
        core = lax.axis_index("section")
        self.owner = core == layer
        self.sibling = {"section": 1 - core}
        self.y, self.z = lax.axis_index("y"), lax.axis_index("z")

    def each(self, run):
        for owner in (True, False):

            @pl.when(self.owner if owner else jnp.logical_not(self.owner))
            def _():
                run(owner)

    @staticmethod
    def parts(owner):
        if owner:
            return [("in", 0, 512, "z"), ("in", 512, 512, "y"), ("out", 0, OUT_SPLIT, "z")]
        return [("in", SPLIT, 512, "z"), ("in", SPLIT + 512, EW - SPLIT - 512, "y"), ("out", OUT_SPLIT, D - OUT_SPLIT, "y")]

    def me(self, axis):
        return self.z if axis == "z" else self.y


def then(axis):
    return "y" if axis == "z" else "z"


def part_rows(kind, half):
    return half_piece(half) if kind == "in" else thirds(half)


class WeightGather(WeightParts):
    def __init__(self, layer, piece, out_piece, lent, lent_out, w_in, w_out, sends, recvs, sib_sends, sib_recvs, lend, local):
        super().__init__(layer)
        self.piece, self.out_piece, self.lent, self.lent_out = piece, out_piece, lent, lent_out
        self.w_in, self.w_out = w_in, w_out
        self.sends, self.recvs, self.sib_sends, self.sib_recvs = sends, recvs, sib_sends, sib_recvs
        self.lend, self.local = lend, local

    def lending(self):
        pairs = ((self.piece.at[:, SPLIT:EW], self.lent), (self.out_piece.at[:, OUT_SPLIT:D], self.lent_out))
        return [remote(a, b, self.lend.at[i], self.lend.at[2 + i], self.sibling) for i, (a, b) in enumerate(pairs)]

    def placing(self, owner):
        y, z = self.y, self.z
        if owner:
            pairs = (
                (self.piece.at[:, 0:SPLIT], self.w_in.at[z, y, :, 0:SPLIT]),
                (self.out_piece.at[:, 0:OUT_SPLIT], self.w_out.at[y, z, :, 0:OUT_SPLIT]),
            )
        else:
            pairs = ((self.lent, self.w_in.at[z, y, :, SPLIT:EW]), (self.lent_out, self.w_out.at[y, z, :, OUT_SPLIT:D]))
        return [pltpu.make_async_copy(a, b, self.local.at[i]) for i, (a, b) in enumerate(pairs)]

    def ones(self, owner):
        rings = []
        for k, (kind, start, width, axis) in enumerate(self.parts(owner)):
            if kind == "in":
                source, shift, where = (self.piece, 0, self.w_in) if owner else (self.lent, SPLIT, self.w_in)
            else:
                source, shift, where = (self.out_piece, 0, self.w_out) if owner else (self.lent_out, OUT_SPLIT, self.w_out)
            lanes = slice(start, start + width)
            near = slice(start - shift, start - shift + width)

            def view(i, h, kind=kind, axis=axis, where=where, lanes=lanes):
                z, y = (i, self.y) if axis == "z" else (self.z, i)
                place = (z, y) if kind == "in" else (y, z)
                return where.at[place[0], place[1], part_rows(kind, h), lanes]

            def own(h, kind=kind, source=source, near=near):
                return source.at[part_rows(kind, h), near]

            rings.append(Ring(axis, view, own, self.sends.at[k], self.recvs.at[k]))
        return rings

    def view(self, part, i, h):
        kind, start, width, axis = part
        lanes = slice(start, start + width)
        where = self.w_in if kind == "in" else self.w_out
        leading = (kind == "in") == (then(axis) == "z")
        return where.at[i, first_two(h), :, lanes] if leading else where.at[first_two(h), i, :, lanes]

    def over(self, owner, k, slot, block, half):
        ref = self.view(self.parts(owner)[k], block, half)
        return remote(ref, ref, self.sib_sends.at[8 * k + slot], self.sib_recvs.at[8 * k + slot], self.sibling)

    def twos(self, owner):
        rings = []
        for k, part in enumerate(self.parts(owner)):
            axis = then(part[3])
            me = self.me(axis)

            def arrived(block, half, slot, k=k):
                self.over(owner, k, slot, block, half).start()

            rings.append(
                Ring(
                    axis, functools.partial(self.view, part), functools.partial(self.view, part, me),
                    self.sends.at[3 + k], self.recvs.at[3 + k], arrived,
                )
            )
        return rings

    def begin(self):
        def run(owner):
            for c in self.lending():
                if owner:
                    c.start()
                else:
                    c.wait_recv()
            for c in self.placing(owner):
                c.start()
            for ring in self.ones(owner):
                ring.start()

        self.each(run)

    def middle(self):
        def run(owner):
            rings = self.ones(owner)
            for ring in rings:
                ring.prepare()
                ring.forward()
            for c in self.placing(owner):
                c.wait()
            for k, (ring, two) in enumerate(zip(rings, self.twos(owner))):
                ring.finish()
                two.start()
                for h in range(2):
                    self.over(owner, k, 6 + h, two.me, h).start()

        self.each(run)

    def pass_on(self):
        def run(owner):
            for ring in self.twos(owner):
                ring.prepare()
                ring.forward()

        self.each(run)

    def finish(self):
        def run(owner):
            for ring in self.twos(owner):
                ring.prepare()
                ring.rebuild()
                ring.finish()

        self.each(run)

    def end(self):
        def run(owner):
            if owner:
                for c in self.lending():
                    c.wait_send()
            for theirs in (False, True):
                role = owner != theirs
                for k, part in enumerate(self.parts(role)):
                    for slot in range(8):
                        half = (0, 1, 1, 0, 0, 1, 0, 1)[slot]
                        c = self.over(role, k, slot, self.me(then(part[3])), half)
                        if theirs:
                            c.wait_recv()
                        else:
                            c.wait_send()

        self.each(run)


def weight_scratch():
    return [
        VMEM((96, EW - SPLIT), bf16), VMEM((48, D - OUT_SPLIT), bf16), sems(6, 6), sems(6, 6), sems(24), sems(24), sems(4),
        sems(2),
    ]


class WeightSum(WeightParts):
    def __init__(self, layer, own, came, rings, whole_in, whole_out, sends, recvs, sib_sends, sib_recvs, local):
        super().__init__(layer)
        self.own, self.came, self.bufs = own, came, rings
        self.whole_in, self.whole_out = whole_in, whole_out
        self.sends, self.recvs, self.sib_sends, self.sib_recvs, self.local = sends, recvs, sib_sends, sib_recvs, local

    def order(self, n, axis):
        me, right, left, across = around(axis)
        return (across, right, left, me)[n]

    @staticmethod
    def block(part, i, grad_in, grad_out):
        kind, start, width, axis = part
        lanes = slice(start, start + width)
        ref = grad_in if kind == "in" else grad_out
        leading = (kind == "in") == (axis == "z")
        return ref.at[i, :, :, lanes] if leading else ref.at[:, i, :, lanes]

    @staticmethod
    def narrow(ref, part):
        width = part[2]
        return ref if ref.shape[-1] == width else ref.at[(slice(None),) * (len(ref.shape) - 1) + (slice(0, width),)]

    def over(self, takes, n, grad_in, grad_out):
        copies = []
        for k, part in enumerate(self.parts(takes)):
            i = self.order(n, part[3])
            copies.append(
                remote(
                    self.block(part, i, grad_in, grad_out), self.narrow(self.came[k].at[i], part),
                    self.sib_sends.at[4 * k + n], self.sib_recvs.at[4 * k + n], self.sibling,
                )
            )
        return copies

    def loads(self, owner, grad_in, grad_out):
        copies = []
        for k, part in enumerate(self.parts(owner)):
            for i in range(4):
                copies.append(
                    pltpu.make_async_copy(
                        self.block(part, i, grad_in, grad_out), self.narrow(self.own[k].at[i], part), self.local.at[4 * k + i]
                    )
                )
        return copies

    def send(self, grad_in, grad_out):
        def run(owner):
            blocks = [self.over(not owner, n, grad_in, grad_out) for n in range(4)]
            for k in range(3):
                for n in range(4):
                    blocks[n][k].start()
            for c in self.loads(owner, grad_in, grad_out):
                c.start()

        self.each(run)

    def sent(self, grad_in, grad_out):
        def run(owner):
            for n in range(4):
                for c in self.over(not owner, n, grad_in, grad_out):
                    c.wait_send()

        self.each(run)

    def add(self, grad_in, grad_out, blocks, first=True):
        def run(owner):
            if first:
                for c in self.loads(owner, grad_in, grad_out):
                    c.wait()
            for n in blocks:
                copies = self.over(owner, n, grad_in, grad_out)
                for k, part in enumerate(self.parts(owner)):
                    copies[k].wait_recv()
                    i = self.order(n, part[3])
                    came = self.narrow(self.came[k].at[i], part)
                    add_tiles(came, self.narrow(self.own[k].at[i], part), came)

        self.each(run)

    def add_and_start(self, grad_in, grad_out):
        def run(owner):
            for c in self.loads(owner, grad_in, grad_out):
                c.wait()
            for k, (part, ring) in enumerate(zip(self.parts(owner), self.ones(owner))):
                for n in range(3):
                    self.over(owner, n, grad_in, grad_out)[k].wait_recv()
                    i = self.order(n, part[3])
                    came = self.narrow(self.came[k].at[i], part)
                    add_tiles(came, self.narrow(self.own[k].at[i], part), came)
                ring.start()

        self.each(run)

    def ones(self, owner):
        rings = []
        for k, part in enumerate(self.parts(owner)):
            landed, relay = self.bufs[2 * k : 2 * k + 2]
            pair = lambda ref: (self.narrow(ref.at[0], part), self.narrow(ref.at[1], part))
            rings.append(
                RingSum(
                    part[3], functools.partial(self.first_view, k, part), pair(landed), pair(relay), self.sends.at[k],
                    self.recvs.at[k],
                )
            )
        return rings

    def first_view(self, k, part, i, h):
        return self.narrow(self.came[k].at[i, first_two(h)], part)

    def second_view(self, k, part, i, h):
        return self.narrow(self.came[k].at[self.me(part[3]), i, part_rows(part[0], h)], part)

    def twos(self, owner):
        rings = []
        for k, part in enumerate(self.parts(owner)):
            bufs = self.bufs[6 + 4 * k : 10 + 4 * k]
            landed, relay = [[self.narrow(ref, part) for ref in refs] for refs in (bufs[0:2], bufs[2:4])]
            rings.append(
                RingSum(
                    then(part[3]), functools.partial(self.second_view, k, part), landed, relay, self.sends.at[3 + k],
                    self.recvs.at[3 + k],
                )
            )
        return rings

    def start_one(self):
        def run(owner):
            for ring in self.ones(owner):
                ring.start()

        self.each(run)

    def forward_one(self):
        def run(owner):
            for ring in self.ones(owner):
                ring.prepare()
                ring.forward()

        self.each(run)

    def finish_one(self):
        def run(owner):
            for k, (part, ring, two) in enumerate(zip(self.parts(owner), self.ones(owner), self.twos(owner))):
                ring.prepare()
                ring.rebuild()
                ring.finish(functools.partial(self.first_view, k, part, self.me(part[3])))
                two.start()

        self.each(run)

    def forward_two(self):
        def run(owner):
            for ring in self.twos(owner):
                ring.prepare()
                ring.forward()

        self.each(run)

    def finish_two(self):
        def run(owner):
            for part, ring in zip(self.parts(owner), self.twos(owner)):
                ring.prepare()
                ring.rebuild()
                whole = self.whole_in if part[0] == "in" else self.whole_out
                lanes = slice(part[1], part[1] + part[2])
                ring.finish(functools.partial(lambda ref, kind, at, h: ref.at[part_rows(kind, h), at], whole, part[0], lanes))

        self.each(run)


def sum_shapes():
    return [(4, 4, 96, 512), (4, 4, 96, 512), (4, 4, 48, OUT_SPLIT)]


def sum_blocks():
    return [VMEM(shape, bf16) for shape in sum_shapes()]


def ring_buffers():
    ones = []
    for rows, width in ((96, 512), (96, 512), (48, OUT_SPLIT)):
        ones += [VMEM((2, 3, 2, rows, width), bf16), VMEM((2, 2, rows, width), bf16)]
    twos = []
    for high, low, width in ((48, 48, 512), (48, 48, 512), (32, 16, OUT_SPLIT)):
        twos += [VMEM((3, high, width), bf16), VMEM((3, low, width), bf16), VMEM((high, width), bf16), VMEM((low, width), bf16)]
    return ones + twos


def ring_halves(*shape):
    return [VMEM((2, 3) + shape, bf16), VMEM((2,) + shape, bf16)]


BUFFERS = 18


def exact(a, b):
    high = a.astype(bf16)
    low = (a - high.astype(f32)).astype(bf16)
    both = dot(jnp.concatenate([high, low], axis=0), b)
    return both[: a.shape[0]] + both[a.shape[0] :]


def as_row(column):
    return jnp.broadcast_to(column, (T, T)).T[0:8, :]


def as_column(row):
    return row.T[:, 0:1]


def heads_to_lanes():
    return expander().astype(bf16)


def lanes_to_heads():
    return jnp.where(iota((XW, 128), 0) // PS == iota((XW, 128), 1), 1.0, 0.0).astype(bf16)


def decay_of(logs, logs_t, h, lower):
    gap = logs[:, h : h + 1] - logs_t[h : h + 1, :]
    return jnp.where(lower, jnp.exp(jnp.minimum(gap, 0.0)), 0.0)


def two_heads(both, left):
    return jnp.concatenate([jnp.where(left, both, 0.0), jnp.where(left, 0.0, both)], axis=0)


def exchange_x(src, slots, sends, recvs):
    x = lax.axis_index("x")
    copies = [
        remote(src, slots.at[d], sends.at[d], recvs.at[d], {"x": lax.rem(x + d + 1, TP)}) for d in range(TP - 1)
    ]
    for c in copies:
        c.start()
    for c in copies:
        c.wait_recv()
    total = src[...] + slots[0] + slots[1] + slots[2]
    for c in copies:
        c.wait_send()
    return total


def mix_peers():
    x = lax.axis_index("x")
    _, right, left, _ = around("y")
    return [{"x": lax.rem(x + d, TP)} for d in range(1, TP)] + [{"y": right}, {"y": left}]


GROUP = 256


def groups(width):
    return [slice(i, i + GROUP) for i in range(0, width, GROUP)]


def vector_views(vecs, layer):
    mine = vecs.at[layer]
    return (
        mine.at[pl.ds(0, K)], mine.at[pl.ds(4, 1)], mine.at[pl.ds(5, 1), pl.ds(0, XW)], mine.at[pl.ds(6, 1), pl.ds(0, XW)],
        mine.at[pl.ds(7, 1), pl.ds(0, 128)], mine.at[pl.ds(8, 1), pl.ds(0, 128)],
    )


def forward_kernel(layer, proj, vecs, normed_two, pre, act, step, cum, states, mixed, scale, decays,
                   increments, wide, end_state, all_states, squares, slots, sends, recvs, x_sends, x_recvs):
    y = lax.axis_index("y")
    cw, cb, gain, skip, rate, bias = vector_views(vecs, layer)
    spread = heads_to_lanes()
    tri = jnp.where(tri_lower(), 1.0, 0.0).astype(f32)
    lower = tri_lower()
    left = pair_mask()
    barrier = greet(mix_peers())
    end_state[...] = jnp.zeros_like(end_state)

    def conv(c, total):
        base = pl.multiple_of(c * T, T)
        rows = pl.ds(base, T)
        for g in groups(UW):
            window = proj[pl.ds(base, T + HALO), XW + g.start : XW + g.stop]
            summed = cb[:, g] + cw[0:1, g] * window[HALO - 3 : HALO - 3 + T]
            for k in range(1, K):
                summed = summed + cw[k : k + 1, g] * window[HALO - 3 + k : HALO - 3 + k + T]
            pre[rows, g] = summed
            act[rows, g] = summed * sigmoid(summed)
        steps = softplus(proj[pl.ds(base + HALO, T), RAW:EW] + bias[...])
        logs = dot(tri, steps * rate[...], FULL)
        step[rows, :] = steps
        cum[rows, :] = logs
        last = logs[T - 1 : T, :]
        whole = jnp.broadcast_to(jnp.exp(last), (16, 128))
        stacked = jnp.concatenate([jnp.exp(last - logs) * steps, jnp.exp(logs), steps, whole], axis=0)
        b_t = act[rows, XW : XW + N].T
        for g in groups(XW):
            spreads = exact(stacked, spread[:, g])
            x = act[rows, g]
            added = dot(b_t, spreads[0:T] * x, ACC)
            increments[c, :, g] = added
            wide[0, rows, g] = spreads[T : 2 * T]
            wide[1, rows, g] = spreads[2 * T : 3 * T] * x
            end_state[:, g] = spreads[3 * T : 3 * T + 1] * end_state[:, g] + added
        return total + last

    total = lax.fori_loop(0, CHUNKS, conv, jnp.zeros((1, 128), f32))
    all_states[y, 0:N, :] = end_state[...]
    all_states[y, N:, :] = exact(jnp.broadcast_to(jnp.exp(total), (16, 128)), spread)
    pl.semaphore_wait(barrier, 5)
    half = (N + 16) // 2
    view = lambda i, h: all_states.at[i, pl.ds(h * half, half)]
    ring = Ring("y", view, lambda h: view(y, h), sends, recvs)
    ring.start()

    def within(c, carry):
        rows = pl.ds(pl.multiple_of(c * T, T), T)
        logs = cum[rows, :]
        logs_t = logs.T
        meet = dot_nt(act[rows, XW + N : UW], act[rows, XW : XW + N], ACC)
        for j in range(HL // 2):
            lanes = slice(128 * j, 128 * (j + 1))
            mats = [decay_of(logs, logs_t, h, lower) * meet for h in (2 * j, 2 * j + 1)]
            part = dot(jnp.concatenate(mats, axis=1), two_heads(wide[1, rows, lanes], left), ACC)
            mixed[rows, lanes] = part + skip[:, lanes] * act[rows, lanes]
        return carry

    lax.fori_loop(0, CHUNKS // 2, within, 0)
    ring.forward()
    lax.fori_loop(CHUNKS // 2, CHUNKS, within, 0)
    ring.finish()
    for g in groups(XW):
        state = jnp.zeros((N, GROUP), f32)
        for i in range(TP - 1):
            decayed = all_states[i, N : N + 1, g] * state + all_states[i, 0:N, g]
            state = jnp.where(y > i, decayed, state)
        states[0, :, g] = state
    for i in range(TP):
        decays[i] = all_states[i, N : N + 8, :]

    def carried(c, carry):
        base = pl.multiple_of(c * T, T)
        rows = pl.ds(base, T)
        cc = act[rows, XW + N : UW]
        sums = jnp.zeros((T, GROUP), f32)
        for g in groups(XW):
            state = states[c, :, g]
            out = mixed[rows, g] + wide[0, rows, g] * dot(cc, state, ACC)
            mixed[rows, g] = out
            z = proj[pl.ds(base + HALO, T), g]
            gated = out * (z * sigmoid(z))
            sums = sums + gated * gated
            states[jnp.minimum(c + 1, CHUNKS - 1), :, g] = jnp.where(
                c < CHUNKS - 1, wide[0, pl.ds(base + T - 8, 8), g][7:8] * state + increments[c, :, g], state
            )
        squares[:, rows] = as_row(jnp.sum(sums, axis=1, keepdims=True))
        return carry

    lax.fori_loop(0, CHUNKS, carried, 0)
    scale[...] = lax.rsqrt(exchange_x(squares, slots, x_sends, x_recvs) * (1.0 / DI) + EPS)

    def norm(c, carry):
        base = pl.multiple_of(c * T, T)
        rows = pl.ds(base, T)
        r = as_column(scale[:, rows])
        for g in groups(XW):
            z = proj[pl.ds(base + HALO, T), g]
            gated = mixed[rows, g] * (z * sigmoid(z))
            normed_two[rows, g] = (gated * r * gain[:, g]).astype(bf16)
        return carry

    lax.fori_loop(0, CHUNKS, norm, 0)


def forward_mix(proj, vecs, layer, collective_id):
    return comm_call(
        functools.partial(forward_kernel, layer),
        [
            ((ROWS, XW), bf16, VMEM), ((ROWS, UW), f32, VMEM), ((ROWS, UW), f32, VMEM), ((ROWS, 128), f32, VMEM),
            ((ROWS, 128), f32, VMEM), ((CHUNKS, N, XW), f32, VMEM), ((ROWS, XW), f32, VMEM), ((8, ROWS), f32, VMEM),
            ((TP, 8, XW), f32, VMEM),
        ],
        [VMEM] * 2,
        [
            VMEM((CHUNKS, N, XW), f32), VMEM((2, ROWS, XW), f32), VMEM((N, XW), f32), VMEM((TP, N + 16, XW), f32),
            VMEM((8, ROWS), f32), VMEM((TP - 1, 8, ROWS), f32), sems(6), sems(6), sems(3), sems(3),
        ],
        collective_id,
        16 * 1024 * 1024,
    )(proj, vecs)


def backward_kernel(layer, late, gn, proj, pre, act, step, cum, states, mixed, scale, decays, vecs, w_in, *more):
    if late:
        sum_a, sum_b, sum_c, gp, partial, vector, late_in, late_out = more[:8]
        more = more[8:]
    else:
        gp, partial, vector = more[:3]
        more = more[3:]
    (conv_grads, bias_grad, gain_grad, dmixed, dpre, within_u, dmeets, all_backs, back_state, head_acc, dots, slots,
     w_here, sends, recvs, x_sends, x_recvs, w_load) = more[:18]
    y = lax.axis_index("y")
    cw, cb, gain, skip, rate, bias = vector_views(vecs, layer)
    spread = heads_to_lanes()
    gather = lanes_to_heads()
    lower = tri_lower()
    upper = jnp.where(iota((T, T), 0) <= iota((T, T), 1), 1.0, 0.0).astype(bf16)
    left = pair_mask()
    w_copy = pltpu.make_async_copy(w_in, w_here, w_load.at[0])
    peers = mix_peers()
    if late:
        came, rings = more[18:21], more[21 : 21 + BUFFERS]
        w_sends, w_recvs, hand_sends, hand_recvs, loads = more[21 + BUFFERS :]
        _, z_right, z_left, _ = around("z")
        sibling = {"section": 1 - lax.axis_index("section")}
        peers = peers + [{"z": z_right}, {"z": z_left}, sibling]
        weights = WeightSum(layer + 1, None, came, rings, late_in, late_out, w_sends, w_recvs, None, None, None)

        loading = [pltpu.make_async_copy(a, b, loads.at[k]) for k, (a, b) in enumerate(zip((sum_a, sum_b, sum_c), came))]
        for c in loading:
            c.start()
    barrier = greet(peers)
    w_copy.start()
    gain_grad[...] = jnp.zeros_like(gain_grad)
    conv_grads[...] = jnp.zeros_like(conv_grads)
    bias_grad[...] = jnp.zeros_like(bias_grad)
    head_acc[...] = jnp.zeros_like(head_acc)
    back_state[...] = jnp.zeros_like(back_state)
    dpre[0:HALO, :] = jnp.zeros((HALO, UW), f32)
    dpre[HALO + ROWS :, :] = jnp.zeros((HALO, UW), f32)
    gp[0:HALO, :] = jnp.zeros((HALO, EW), bf16)

    def row_sums(c, carry):
        base = pl.multiple_of(c * T, T)
        rows = pl.ds(base, T)
        r = as_column(scale[:, rows])
        sums = jnp.zeros((T, GROUP), f32)
        for g in groups(XW):
            z = proj[pl.ds(base + HALO, T), g]
            product = gn[rows, g] * (mixed[rows, g] * (z * sigmoid(z)))
            gain_grad[:, g] += jnp.sum(product * r, axis=0, keepdims=True)
            sums = sums + product * gain[:, g]
        dots[:, rows] = as_row(jnp.sum(sums, axis=1, keepdims=True))
        return carry

    lax.fori_loop(0, CHUNKS, row_sums, 0)
    pl.semaphore_wait(barrier, len(peers))
    if late:
        for c in loading:
            c.wait()
        weights.start_one()
    dots[...] = exchange_x(dots, slots, x_sends, x_recvs)

    def gate_back(c, offset):
        base = pl.multiple_of(c * T, T)
        rows = pl.ds(base, T)
        r = as_column(scale[:, rows])
        pull = r * r * r * (as_column(dots[:, rows]) * (1.0 / DI))
        logs = cum[rows, :]
        decay = jnp.exp(logs + offset).astype(bf16)
        cc_t = act[rows, XW + N : UW].T.astype(bf16)
        for g in groups(XW):
            out = mixed[rows, g]
            z = proj[pl.ds(base + HALO, T), g]
            sig = sigmoid(z)
            silu = z * sig
            dgated = r * (gn[rows, g] * gain[:, g]) - (out * silu) * pull
            dy = dgated * silu
            dmixed[rows, g] = dy
            gp[pl.ds(base + HALO, T), g] = (dgated * out * (sig + silu * (1.0 - sig))).astype(bf16)
            back_state[:, g] += dot(cc_t, (dot(decay, spread[:, g]) * dy).astype(bf16))
        return offset + logs[T - 1 : T, :]

    lax.fori_loop(0, CHUNKS, gate_back, jnp.zeros((1, 128), f32))
    all_backs[y] = back_state[...].astype(bf16)
    view = lambda i, h: all_backs.at[i, pl.ds(h * (N // 2), N // 2)]
    ring = Ring("y", view, lambda h: view(y, h), sends, recvs)
    ring.start()

    def within(c, carry):
        rows = pl.ds(pl.multiple_of(c * T, T), T)
        logs = cum[rows, :]
        logs_t = logs.T
        b = act[rows, XW : XW + N].astype(bf16)
        cc = act[rows, XW + N : UW].astype(bf16)
        steps = step[rows, :].astype(bf16)
        meet = dot_nt(cc, b)
        dmeet = jnp.zeros((T, T), f32)
        for j in range(HL // 2):
            lanes = slice(128 * j, 128 * (j + 1))
            scaled = (act[rows, lanes] * dot(steps, spread[:, lanes])).astype(bf16)
            stacked = two_heads(dmixed[rows, lanes], left).astype(bf16)
            dmats = dot_nt(stacked, scaled)
            mats = []
            for k in range(2):
                decay = decay_of(logs, logs_t, 2 * j + k, lower)
                mats.append((decay * meet).astype(bf16))
                dmeet = dmeet + decay * dmats[k * T : (k + 1) * T, :]
            within_u[rows, lanes] = dot_tn(jnp.concatenate(mats, axis=0), stacked)
        dmeets[c] = dmeet.astype(bf16)
        return carry

    lax.fori_loop(0, CHUNKS // 2, within, 0)
    ring.forward()
    if late:
        weights.forward_one()
    lax.fori_loop(CHUNKS // 2, CHUNKS, within, 0)
    ring.finish()
    if late:
        weights.finish_one()
    for g in groups(XW):
        grad = jnp.zeros((N, GROUP), f32)
        for i in range(TP - 1, 0, -1):
            decayed = decays[i, 0:1, g] * grad + all_backs[i, :, g].astype(f32)
            grad = jnp.where(y < i, decayed, grad)
        back_state[:, g] = grad

    def chunk(i, carry):
        c = CHUNKS - 1 - i
        base = pl.multiple_of(c * T, T)
        rows = pl.ds(base, T)
        later = pl.ds(base + HALO, T)
        steps = step[rows, :]
        logs = cum[rows, :]
        last = logs[T - 1 : T, :]
        b = act[rows, XW : XW + N].astype(bf16)
        cc_full = act[rows, XW + N : UW]
        cc = cc_full.astype(bf16)
        cc_t = cc_full.T.astype(bf16)
        whole = jnp.broadcast_to(jnp.exp(last), (16, 128))
        step_rows = jnp.concatenate([steps, whole], axis=0)
        decay_rows = jnp.concatenate([jnp.exp(last - logs), jnp.exp(logs)], axis=0).astype(bf16)
        dmeet = dmeets[c]
        dcc = dot(dmeet, b)
        db = dot_tn(dmeet, cc)
        sums = jnp.zeros((3 * T, 128), f32)
        tail_heads = jnp.zeros((16, 128), f32)
        for g in groups(XW):
            x = act[rows, g]
            dy = dmixed[rows, g]
            out = mixed[rows, g] - skip[:, g] * x
            state = states[c, :, g]
            dstate = back_state[:, g]
            dstate_low = dstate.astype(bf16)
            spreads = exact(step_rows, spread[:, g])
            step_wide = spreads[0:T]
            last_wide = spreads[T : T + 1]
            lows = dot(decay_rows, spread[:, g])
            after_wide = lows[0:T]
            scaled = (x * step_wide).astype(bf16).astype(f32)
            entered = (lows[T:] * dy).astype(bf16)
            arriving = after_wide * dot(b, dstate_low)
            u = within_u[rows, g] + arriving
            s = pre[rows, g]
            sig = sigmoid(s)
            dpre[later, g] = (step_wide * u + skip[:, g] * dy) * (sig + s * sig * (1.0 - sig))
            sums = sums + exact(
                jnp.concatenate([dy.astype(bf16).astype(f32) * out - scaled * u, x * u, dy * x], axis=0), gather[g, :]
            )
            tail = jnp.sum(dstate * (last_wide * state), axis=0, keepdims=True)
            tail = tail + jnp.sum(arriving * scaled, axis=0, keepdims=True)
            tail_heads = tail_heads + exact(jnp.broadcast_to(tail, (16, GROUP)), gather[g, :])
            dcc = dcc + dot_nt(entered, state.astype(bf16))
            db = db + dot_nt((after_wide * scaled).astype(bf16), dstate_low)
            back_state[:, g] = dot(cc_t, entered) + last_wide * dstate
        dsum = sums[0:T]
        high = dsum.astype(bf16)
        low = (dsum - high.astype(f32)).astype(bf16)
        da = dot(upper, high) + dot(upper, low) + tail_heads[0:1, :]
        dstep = sums[T : 2 * T] + da * rate[...]
        raw = proj[later, RAW:EW] + bias[...]
        draw = jnp.where(iota((T, 128), 1) < HL, dstep * sigmoid(raw), 0.0)
        head_acc[0:1, :] += jnp.sum(da * steps, axis=0, keepdims=True) * rate[...]
        head_acc[1:2, :] += jnp.sum(sums[2 * T :], axis=0, keepdims=True)
        head_acc[2:3, :] += jnp.sum(draw, axis=0, keepdims=True)
        gp[later, RAW:EW] = draw.astype(bf16)
        for lanes, value in ((slice(XW, XW + N), db), (slice(XW + N, UW), dcc)):
            s = pre[rows, lanes]
            sig = sigmoid(s)
            dpre[later, lanes] = value * (sig + s * sig * (1.0 - sig))
        return carry

    lax.fori_loop(0, CHUNKS // 2, chunk, 0)
    if late:
        weights.forward_two()
    lax.fori_loop(CHUNKS // 2, CHUNKS, chunk, 0)
    if late:
        weights.finish_two()
        handing = [
            remote(ref, ref, hand_sends.at[k], hand_recvs.at[k], sibling)
            for k, ref in enumerate((late_in.at[:, SPLIT:EW], late_out.at[:, OUT_SPLIT:D]))
        ]

        @pl.when(jnp.logical_not(weights.owner))
        def _():
            for c in handing:
                c.start()

    def conv(c, carry):
        base = pl.multiple_of(c * T, T)
        for g in groups(UW):
            window = proj[pl.ds(base, T + HALO), XW + g.start : XW + g.stop]
            grads = dpre[pl.ds(base + HALO, T + HALO), g]
            own = grads[0:T]
            du = cw[K - 1 : K, g] * own
            for k in range(K - 1):
                du = du + cw[k : k + 1, g] * grads[K - 1 - k : K - 1 - k + T]
            gp[pl.ds(base + HALO, T), XW + g.start : XW + g.stop] = du.astype(bf16)
            for k in range(K):
                conv_grads[k : k + 1, g] += jnp.sum(
                    own * window[HALO - 3 + k : HALO - 3 + k + T], axis=0, keepdims=True
                )
            bias_grad[:, g] += jnp.sum(own, axis=0, keepdims=True)
        return carry

    lax.fori_loop(0, CHUNKS, conv, 0)
    first = dpre[0 : 2 * HALO, :]
    du = jnp.zeros((HALO, UW), f32)
    for k in range(K - 1):
        du = du + cw[k : k + 1, :] * first[K - 1 - k : K - 1 - k + HALO]
    gp[0:HALO, XW:RAW] = du.astype(bf16)
    w_copy.wait()

    def project(n, carry):
        at = pl.ds(pl.multiple_of(n * GROUP, GROUP), GROUP)
        partial[:, at] = dot_nt(gp[...], w_here[at, :]).astype(bf16)
        return carry

    lax.fori_loop(0, D // GROUP, project, 0)
    vector[...] = jnp.zeros_like(vector)
    vector[2 : 2 + K, :] = conv_grads[:, 0:XW]
    vector[6:7, :] = bias_grad[:, 0:XW]
    vector[7:8, :] = gain_grad[...]
    vector[8 : 8 + K, 0 : 2 * N] = conv_grads[:, XW:UW]
    vector[12:13, 0 : 2 * N] = bias_grad[:, XW:UW]
    vector[13:16, 0:128] = head_acc[0:3, :]
    if late:

        @pl.when(weights.owner)
        def _():
            for c in handing:
                c.wait_recv()

        @pl.when(jnp.logical_not(weights.owner))
        def _():
            for c in handing:
                c.wait_send()


def backward_mix(gn, proj, kept, vecs, w_in, layer, sums, collective_id):
    late = sums is not None
    outs = [((EXT, EW), bf16, VMEM), ((EXT, D), bf16, VMEM), ((16, XW), f32, VMEM)]
    scratch = [
        VMEM((K, UW), f32), VMEM((1, UW), f32), VMEM((1, XW), f32),
        VMEM((ROWS, XW), f32), VMEM((ROWS + 2 * HALO, UW), f32), VMEM((ROWS, XW), f32), VMEM((CHUNKS, T, T), bf16),
        VMEM((TP, N, XW), bf16), VMEM((N, XW), f32), VMEM((8, 128), f32), VMEM((8, ROWS), f32),
        VMEM((TP - 1, 8, ROWS), f32), VMEM((D, EW), bf16), sems(6), sems(6), sems(3), sems(3), sems(1),
    ]
    if late:
        outs += [((96, EW), f32, VMEM), ((48, D), f32, VMEM)]
        scratch += [*sum_blocks(), *ring_buffers(), sems(6, 6), sems(6, 6), sems(2), sems(2), sems(3)]
    return comm_call(
        functools.partial(backward_kernel, layer, late),
        outs,
        [VMEM] * 11 + [ANY] * (4 if late else 1),
        scratch,
        collective_id,
        16 * 1024 * 1024,
    )(gn, proj, *kept, vecs, w_in, *(sums if late else ()))


def collect_kernel(in_rows, out_piece, norm, conv, conv_bias, gate, decay, skip, bias, entering, given, zeros,
                   own_in, own_out, w_in, w_out, vectors, heads, entering_all, given_all,
                   pieces, landing, wide, staged, small, head_rows, local, x_sends, x_recvs, swap_sends, swap_recvs,
                   v_sends, v_recvs, sends, recvs, halo_sends, halo_recv, sib_sends, sib_recvs, *weights):
    core = lax.axis_index("section")
    x, x_right, x_left, x_across = around("x")
    y, y_right, y_left, _ = around("y")
    z, z_right, z_left, _ = around("z")
    sibling = {"section": 1 - core}
    peers = [{"x": lax.rem(x + d, TP)} for d in range(1, TP)]
    swap = {"z": x, "x": z}
    off_diagonal = z != x
    barrier = greet(peers + [{"y": y_right}, {"y": y_left}, {"z": z_right}, {"z": z_left}, sibling])
    greet_rows(barrier)

    @pl.when(off_diagonal)
    def _():
        pl.semaphore_signal(barrier, inc=1, device_id=swap, device_id_type=MESH)

    tail = in_rows[:, 2 * DI + 2 * N :].astype(f32)
    for i in range(TP):
        pieces[i, :, 0:XW] = in_rows[:, i * XW : (i + 1) * XW]
        pieces[i, :, XW : 2 * XW] = in_rows[:, DI + i * XW : DI + (i + 1) * XW]
        pieces[i, :, 2 * XW : RAW] = in_rows[:, 2 * DI : 2 * DI + 2 * N]
        turned = tail if i == 0 else pltpu.roll(tail, 128 - i * HL, 1)
        pieces[i, :, RAW:EW] = jnp.where(iota((24, 128), 1) < HL, turned, 0.0).astype(bf16)
    small[...] = jnp.zeros_like(small)
    small[0:1, 0:24] = norm[...].astype(f32)
    small[1:5, 0:52] = conv[...].astype(f32)
    small[5:6, 0:52] = conv_bias[...].astype(f32)
    small[6:7, 0:48] = gate[...].astype(f32)
    head_rows[...] = jnp.zeros_like(head_rows)
    head_rows[0:1, 0:H] = decay[...]
    head_rows[1:2, 0:H] = skip[...]
    head_rows[2:3, 0:H] = bias[...]
    wait_counts(barrier, 8, (off_diagonal, 1), (givers()[0], TP))

    shares = []
    for i, peer in enumerate(peers):
        shares.append(remote(pieces.at[peer["x"]], landing.at[x], x_sends.at[i], x_recvs.at[x], peer))
        shares.append(remote(small, vectors.at[core, z, y, x], v_sends.at[i], v_recvs.at[x], peer))
    for c in shares:
        c.start()
    swapping = remote(out_piece, own_out, swap_sends.at[0], swap_recvs.at[0], swap)
    stay = pltpu.make_async_copy(out_piece, own_out, local.at[0])

    @pl.when(off_diagonal)
    def _():
        swapping.start()

    @pl.when(jnp.logical_not(off_diagonal))
    def _():
        stay.start()
        stay.wait()

    mine = pltpu.make_async_copy(small, vectors.at[core, z, y, x], local.at[1])
    mine.start()
    head_copy = pltpu.make_async_copy(head_rows, heads.at[core], local.at[2])
    head_copy.start()
    head_over = remote(head_rows, heads.at[core], sib_sends.at[1], sib_recvs.at[1], sibling)
    head_over.start()
    wide[pl.ds(pl.multiple_of(x * 24, 8), 24), :] = pieces[x].astype(f32)
    for i in range(1, TP):
        j = lax.rem(x + i, TP)
        remote(pieces.at[x], landing.at[j], x_sends.at[0], x_recvs.at[j], peers[0]).wait_recv()
        wide[pl.ds(pl.multiple_of(j * 24, 8), 24), :] = landing[j].astype(f32)
        remote(small, vectors.at[core, z, y, j], v_sends.at[0], v_recvs.at[j], peers[0]).wait_recv()
    staged[...] = wide[...].astype(bf16)
    mine.wait()
    keep = pltpu.make_async_copy(staged, own_in, local.at[3])
    keep.start()

    @pl.when(off_diagonal)
    def _():
        swapping.wait_recv()

    gather = WeightGather(0, staged, own_out, weights[0], weights[1], w_in, w_out, *weights[2:])
    gather.begin()
    rows_in = RowGather(
        entering, entering_all, True, sends.at[0], recvs.at[0], local.at[pl.ds(4, 2)], halo_sends, halo_recv, zeros
    )
    rows_given = RowGather(given, given_all, False, sends.at[1], recvs.at[1], local.at[pl.ds(6, 2)])
    rows_in.start()
    rows_given.start()

    def vector_ring(axis, view, base):
        own = y if axis == "y" else z
        return Ring(axis, view, lambda h: view(own, h), sends.at[base], recvs.at[base])

    small_y = vector_ring("y", lambda i, h: vectors.at[core, z, i, first_two(h)], 2)
    small_z = vector_ring("z", lambda i, h: vectors.at[core, i, first_two(h)], 3)
    small_y.start()
    gather.middle()
    small_y.forward()
    small_y.finish()
    small_z.start()
    rows_in.forward()
    gather.pass_on()
    small_z.forward()
    rows_given.forward()
    small_z.finish()
    over = remote(vectors.at[core], vectors.at[core], sib_sends.at[0], sib_recvs.at[0], sibling)
    over.start()
    rows_in.finish()
    gather.finish()
    rows_given.finish()
    gather.end()
    other = vectors.at[1 - core]
    remote(other, other, sib_sends.at[0], sib_recvs.at[0], sibling).wait_recv()
    remote(head_rows, heads.at[1 - core], sib_sends.at[1], sib_recvs.at[1], sibling).wait_recv()
    over.wait_send()
    head_over.wait_send()
    head_copy.wait()
    keep.wait()
    for c in shares:
        c.wait_send()

    @pl.when(off_diagonal)
    def _():
        swapping.wait_send()


def collect(in_rows, small, entering, given, collective_id):
    return comm_call(
        collect_kernel,
        [
            ((96, EW), bf16, ANY), ((48, D), bf16, VMEM), ((4, 4, 96, EW), bf16, ANY), ((4, 4, 48, D), bf16, ANY),
            ((2, 4, 4, 4, 8, 128), f32, ANY), ((2, 8, 128), f32, ANY), ((EXT, D), bf16, ANY), ((ROWS, D), bf16, ANY),
        ],
        [VMEM] * 9 + [ANY] * 3,
        [
            VMEM((TP, 24, EW), bf16), VMEM((TP, 24, EW), bf16), VMEM((96, EW), f32), VMEM((96, EW), bf16),
            VMEM((8, 128), f32), VMEM((8, 128), f32), sems(8), sems(3), sems(4), sems(1), sems(1), sems(3), sems(4),
            sems(4, 6), sems(4, 6), sems(TP), sems(1), sems(2), sems(2), *weight_scratch(),
        ],
        collective_id,
        16 * 1024 * 1024,
    )(in_rows, *small, entering, given, jnp.zeros((HALO, D), bf16))


def relay_forward_kernel(part, series, valid, gain, own_in, own_out, zeros, handed, normed_all, w_in, w_out,
                         total, normed, landed, relay, sum_sends, sum_recvs, row_sends, row_recvs, halo_sends, halo_recv,
                         local, *weights):
    x, x_right, x_left, _ = around("x")
    y, y_right, y_left, _ = around("y")
    z, z_right, z_left, _ = around("z")
    sibling = {"section": 1 - lax.axis_index("section")}
    barrier = greet(
        [{"x": x_right}, {"x": x_left}, {"y": y_right}, {"y": y_left}, {"z": z_right}, {"z": z_left}, sibling]
    )
    greet_rows(barrier)
    wait_counts(barrier, 7, (givers()[0], TP))
    sums = RowSum(part, False, landed, relay, sum_sends, sum_recvs)
    gather = WeightGather(1, own_in, own_out, weights[0], weights[1], w_in, w_out, *weights[2:])
    sums.start()
    gather.begin()
    gather.middle()
    sums.forward()
    gather.pass_on()
    sums.finish(total)
    low = (valid[...] * (series[...].astype(f32) + total[...])).astype(bf16)
    handed[...] = low
    values = low.astype(f32)
    normed[...] = (values * row_scale(values) * gain[1:2, :]).astype(bf16)
    rows = RowGather(normed, normed_all, True, row_sends, row_recvs, local, halo_sends, halo_recv, zeros)
    rows.start()
    rows.forward()
    gather.finish()
    rows.finish()
    gather.end()


def relay_forward(part, series, valid, gain, own_in, own_out, collective_id):
    return comm_call(
        relay_forward_kernel,
        [((T, D), bf16, VMEM), ((EXT, D), bf16, ANY), ((4, 4, 96, EW), bf16, ANY), ((4, 4, 48, D), bf16, ANY)],
        [VMEM] * 6 + [ANY],
        [
            VMEM((T, D), f32), VMEM((T, D), bf16), VMEM((2, 3, HALF, D), f32), VMEM((2, HALF, D), f32),
            sems(6), sems(6), sems(6), sems(6), sems(TP), sems(1), sems(2), *weight_scratch(),
        ],
        collective_id,
        16 * 1024 * 1024,
    )(part, series, valid, gain, own_in, own_out, jnp.zeros((HALO, D), bf16))


def norm_backward(gnormed, series, gain, gout):
    r = row_scale(series)
    dv = gnormed * gain
    grad = r * dv - series * (r * r * r) * jnp.mean(dv * series, axis=-1, keepdims=True) + gout
    return grad, jnp.sum(gnormed * series * r, axis=0, keepdims=True)


def relay_backward_kernel(part, middle, valid, gain, gout, grad_in, grad_out, grad, norm_grad, rows_all, sum_a, sum_b, sum_c,
                          total, low, landed, relay, edges, *more):
    own, came = more[0:3], more[3:6]
    (sum_sends, sum_recvs, edge_send, edge_recvs, row_sends, row_recvs, local, sib_sends, sib_recvs, loads, stores) = more[6:]
    x, x_right, x_left, _ = around("x")
    sibling = {"section": 1 - lax.axis_index("section")}
    barrier = greet([{"x": x_right}, {"x": x_left}, sibling])
    greet_edges(barrier)
    wait_counts(barrier, 3, (givers()[1], 1))
    sums = RowSum(part, True, landed, relay, sum_sends, sum_recvs, edges, edge_send, edge_recvs)
    weights = WeightSum(1, own, came, None, None, None, None, None, sib_sends, sib_recvs, loads)

    @pl.when(jnp.logical_not(weights.owner))
    def _():
        came[1][:, :, :, EW - SPLIT - 512 : 512] = jnp.zeros((4, 4, 96, 1024 + SPLIT - EW), bf16)

    sums.start()
    weights.send(grad_in, grad_out)
    sums.forward()
    sums.finish(total)
    value, norm = norm_backward(total[...], middle[...].astype(f32), gain[1:2, :], gout[...].astype(f32))
    grad[...] = value
    norm_grad[...] = norm
    low[...] = (valid[...] * value.astype(bf16).astype(f32)).astype(bf16)
    rows = RowGather(low, rows_all, False, row_sends, row_recvs, local)
    rows.start()
    rows.forward()
    weights.add(grad_in, grad_out, range(4))

    keeping = [
        pltpu.make_async_copy(a, b, stores.at[k]) for k, (a, b) in enumerate(zip(came, (sum_a, sum_b, sum_c)))
    ]
    for c in keeping:
        c.start()
    rows.finish()
    weights.sent(grad_in, grad_out)
    for c in keeping:
        c.wait()


def relay_backward(part, middle, valid, gain, gout, grad_in, grad_out, collective_id):
    return comm_call(
        relay_backward_kernel,
        [
            ((T, D), f32, VMEM), ((1, D), f32, VMEM), ((ROWS, D), bf16, ANY),
            *[(shape, bf16, ANY) for shape in sum_shapes()],
        ],
        [VMEM] * 5 + [ANY] * 2,
        [
            VMEM((T, D), f32), VMEM((T, D), bf16), VMEM((2, 3, HALF, D), bf16), VMEM((2, HALF, D), bf16),
            VMEM((TP, HALO, D), bf16), *sum_blocks(), *sum_blocks(), sems(6), sems(6), sems(1), sems(TP), sems(6), sems(6),
            sems(2), sems(12), sems(12), sems(12), sems(3),
        ],
        collective_id,
        16 * 1024 * 1024,
    )(part, middle, valid, gain, gout, grad_in, grad_out)


def own_columns(buffer, row, count, width, place):
    start = place * width
    base = lax.div(start, 128) * 128
    window = buffer[:, pl.ds(pl.multiple_of(base, 128), 256)]
    turned = pltpu.roll(window, lax.rem(256 - (start - base), 256), 1)
    return turned[row : row + count, 0:width]


def settle_kernel(grad_in, grad_out, vector_first, vector_second, norm_second, late_in, late_out, last_part, first_part,
                  entering, handed, valid, gain, grad_second, out_in, out_out, out_norm, out_conv, out_bias, out_gate,
                  out_decay, out_skip, out_step, out_acts, out_grads,
                  whole_in, whole_out, landing, v_all, v_in, v_slots, v_out, v_conv, v_other, p1, p1s, q1, q1s, edges, total,
                  grad_first, second, sib_sends, sib_recvs, sends, recvs, v_sends, v_recvs, x_sends, x_recvs, b_sends,
                  b_recvs, swap_sends, swap_recvs, edge_send, edge_recvs, w_sends, w_recvs, w_sib_sends, w_sib_recvs, loads,
                  *blocks):
    core = lax.axis_index("section")
    x, x_right, x_left, x_across = around("x")
    y = lax.axis_index("y")
    z = lax.axis_index("z")
    sibling = {"section": 1 - core}
    off_diagonal = z != x
    others = [lax.rem(x + d, TP) for d in range(1, TP)]
    x_peers = [{"x": j} for j in others]
    y_peers = [{"y": lax.rem(y + d, TP)} for d in range(1, TP)]
    z_peers = [{"z": lax.rem(z + d, TP)} for d in range(1, TP)]
    barrier = greet(x_peers + y_peers + z_peers + [sibling])
    greet_edges(barrier)

    @pl.when(off_diagonal)
    def _():
        pl.semaphore_signal(barrier, inc=1, device_id={"section": 1, "z": x, "x": z}, device_id_type=MESH)

        @pl.when(core == 0)
        def _():
            pl.semaphore_signal(barrier, inc=1, device_id={"section": 0, "z": x, "x": z}, device_id_type=MESH)

    @pl.when(core == 0)
    def _():
        for j in others:
            pl.semaphore_signal(barrier, inc=1, device_id={"section": 1, "x": j}, device_id_type=MESH)

    v_all[0] = vector_first[...]
    v_all[1] = vector_second[...]
    v_all[1, 0:1, :] = norm_second[:, 0:XW]
    v_all[1, 1:2, :] = norm_second[:, XW:D]
    wait_counts(
        barrier, 10, (core == 1, 3), (off_diagonal, 1), (jnp.logical_and(core == 1, off_diagonal), 1), (givers()[1], 1)
    )

    def beside(src, dst, slot):
        return remote(src, dst, sib_sends.at[slot], sib_recvs.at[slot], sibling)

    weights = WeightSum(
        0, blocks[0:3], blocks[3:6], blocks[6:], whole_in, whole_out, w_sends, w_recvs, w_sib_sends, w_sib_recvs, loads
    )
    sum_first = RowSum(first_part, True, q1, q1s, sends.at[1], recvs.at[1], edges, edge_send, edge_recvs)
    sum_last = RowSum(last_part, False, p1, p1s, sends.at[0], recvs.at[0])
    weights.send(grad_in, grad_out)
    sum_first.start()
    act_first = beside(handed, out_acts.at[core], 0)
    act_second = beside(second, out_acts.at[core], 0)
    grad_over_first = beside(grad_first, out_grads.at[core], 1)
    grad_over_second = beside(grad_second, out_grads.at[core], 1)

    sum_first.forward()
    weights.add_and_start(grad_in, grad_out)
    sum_first.finish(total)
    value, norm = norm_backward(
        total[...], entering[...].astype(f32), gain[0:1, :],
        valid[...] * grad_second[...].astype(bf16).astype(f32),
    )
    grad_first[...] = value
    v_all[0, 0:1, :] = norm[:, 0:XW]
    v_all[0, 1:2, :] = norm[:, XW:D]
    vec = remote(v_all.at[1 - core], v_slots.at[0], v_sends.at[0], v_recvs.at[0], sibling)
    vec.start()
    weights.add(grad_in, grad_out, (3,), first=False)
    sum_last.start()

    @pl.when(core == 1)
    def _():
        act_first.start()
        grad_over_first.start()
        out_grads[1] = grad_second[...]

    @pl.when(core == 0)
    def _():
        grad_over_second.start()
        out_grads[0] = value
        out_acts[0] = handed[...]

    vec.wait_recv()
    v_in[0] = v_all[core] + v_slots[0]

    def spread_vector(stage, peers):
        base = 1 + 3 * stage
        copies = [
            remote(v_in.at[stage], v_slots.at[base + i], v_sends.at[base + i], v_recvs.at[base + i], peer)
            for i, peer in enumerate(peers)
        ]
        for c in copies:
            c.start()
        return copies

    def sum_vector(stage, copies):
        base = 1 + 3 * stage
        for c in copies:
            c.wait_recv()
        v_in[stage + 1] = v_in[stage] + v_slots[base] + v_slots[base + 1] + v_slots[base + 2]
        for c in copies:
            c.wait_send()

    spreading = spread_vector(0, y_peers)
    weights.forward_one()
    sum_vector(0, spreading)
    spreading = spread_vector(1, z_peers)
    sum_last.forward()
    weights.finish_one()
    sum_vector(1, spreading)
    vector_copies = [
        remote(v_in.at[2], v_out.at[x], v_sends.at[7 + i], v_recvs.at[7 + x], peer) for i, peer in enumerate(x_peers)
    ]
    for c in vector_copies:
        c.start()
    v_out[x] = v_in[2]
    weights.forward_two()

    sum_last.finish(total)
    second[...] = (valid[...] * (handed[...].astype(f32) + total[...])).astype(bf16)

    @pl.when(core == 0)
    def _():
        act_second.start()

    @pl.when(core == 1)
    def _():
        out_acts[1] = second[...]

    weights.finish_two()

    def rows_of(j):
        return pl.ds(pl.multiple_of(j * 24, 8), 24)

    def shared(source, lanes, i, where):
        ref = source.at[rows_of(others[i]), lanes]
        return remote(ref, landing.at[x, :, lanes], x_sends.at[i], x_recvs.at[x], where)

    first_lanes, later_lanes = slice(0, SPLIT), slice(SPLIT, EW)
    mine = [shared(whole_in, first_lanes, i, x_peers[i]) for i in range(TP - 1)]
    late = [shared(late_in, slice(0, EW), i, x_peers[i]) for i in range(TP - 1)]
    across_cores = [
        remote(
            whole_in.at[rows_of(j), later_lanes], landing.at[x, :, later_lanes], b_sends.at[d], b_recvs.at[x],
            {"section": 0, "x": j},
        )
        for d, j in enumerate([x] + others)
    ]
    place_back = {"section": 0, "z": x, "x": z}
    out_first, out_later = slice(0, OUT_SPLIT), slice(OUT_SPLIT, D)
    out_near = remote(whole_out.at[:, out_first], out_out.at[:, out_first], swap_sends.at[1], swap_recvs.at[1], place_back)
    out_over = remote(whole_out.at[:, out_later], out_out.at[:, out_later], swap_sends.at[0], swap_recvs.at[0], place_back)
    out_late = remote(late_out, out_out, swap_sends.at[1], swap_recvs.at[0], {"section": 1, "z": x, "x": z})

    @pl.when(core == 0)
    def _():
        for c in mine:
            c.start()
        landing[x, :, first_lanes] = whole_in[rows_of(x), first_lanes]

        @pl.when(off_diagonal)
        def _():
            out_near.start()

        @pl.when(jnp.logical_not(off_diagonal))
        def _():
            out_out[:, out_first] = whole_out[:, out_first]

    @pl.when(core == 1)
    def _():
        for c in across_cores:
            c.start()
        out_over.start()
        for c in late:
            c.start()
        landing[x] = late_in[rows_of(x), :]

        @pl.when(off_diagonal)
        def _():
            out_late.start()

        @pl.when(jnp.logical_not(off_diagonal))
        def _():
            out_out[...] = late_out[...]

    for j in others:
        remote(v_in.at[2], v_out.at[j], v_sends.at[7], v_recvs.at[7 + j], x_peers[0]).wait_recv()
    v_conv[...] = jnp.zeros_like(v_conv)
    v_other[...] = jnp.zeros_like(v_other)
    heads = jnp.zeros((3, 128), f32)
    for i in range(TP):
        v_conv[0 : K + 1, i * XW : (i + 1) * XW] = v_out[i, 2:7, :]
        v_other[1:2, i * XW : (i + 1) * XW] = v_out[i, 7:8, :]
        block = v_out[i, 8:16, 0:128]
        block = jnp.where(iota((8, 128), 1) < HL, block, 0.0)
        heads = heads + (block if i == 0 else pltpu.roll(block, i * HL, 1))[5:8]
    v_conv[0 : K + 1, DI:CONV] = (
        v_out[0, 8:13, 0 : 2 * N] + v_out[1, 8:13, 0 : 2 * N] + v_out[2, 8:13, 0 : 2 * N] + v_out[3, 8:13, 0 : 2 * N]
    )
    norms = v_out[0, 0:2, :] + v_out[1, 0:2, :] + v_out[2, 0:2, :] + v_out[3, 0:2, :]
    v_other[0:1, 0:XW] = norms[0:1]
    v_other[0:1, XW:D] = norms[1:2]
    place = z * 16 + y * 4 + x
    conv = own_columns(v_conv, 0, K + 1, 52, place)
    out_conv[...] = conv[0:K]
    out_bias[...] = conv[K : K + 1]
    out_norm[...] = own_columns(v_other, 0, 1, 24, place)
    out_gate[...] = own_columns(v_other, 1, 1, 48, place)
    out_decay[...] = heads[0:1, 0:H]
    out_skip[...] = heads[1:2, 0:H]
    out_step[...] = heads[2:3, 0:H]

    @pl.when(core == 0)
    def _():
        for j in others:
                remote(
                whole_in.at[rows_of(x), first_lanes], landing.at[j, :, first_lanes], x_sends.at[0], x_recvs.at[j], x_peers[0]
            ).wait_recv()
        for j in range(TP):
            remote(
                whole_in.at[rows_of(x), later_lanes], landing.at[j, :, later_lanes], b_sends.at[0], b_recvs.at[j], sibling
            ).wait_recv()
        out_over.wait_recv()

        @pl.when(off_diagonal)
        def _():
            out_near.wait_recv()

    @pl.when(core == 1)
    def _():
        for j in others:
            remote(late_in.at[rows_of(x)], landing.at[j], x_sends.at[0], x_recvs.at[j], x_peers[0]).wait_recv()

        @pl.when(off_diagonal)
        def _():
            out_late.wait_recv()

    both = jnp.zeros((24, 2 * N), f32)
    steps = jnp.zeros((24, 128), f32)
    for i in range(TP):
        out_in[:, i * XW : (i + 1) * XW] = landing[i, :, 0:XW]
        out_in[:, DI + i * XW : DI + (i + 1) * XW] = landing[i, :, XW : 2 * XW]
        both = both + landing[i, :, 2 * XW : RAW]
        block = jnp.where(iota((24, 128), 1) < HL, landing[i, :, RAW:EW], 0.0)
        steps = steps + (block if i == 0 else pltpu.roll(block, i * HL, 1))
    out_in[:, 2 * DI : 2 * DI + 2 * N] = both
    out_in[:, 2 * DI + 2 * N : E] = steps[:, 0:H]

    weights.sent(grad_in, grad_out)

    @pl.when(core == 0)
    def _():
        grad_over_second.wait_send()
        act_second.wait_send()
        for c in mine:
            c.wait_send()

        @pl.when(off_diagonal)
        def _():
            out_near.wait_send()

    @pl.when(core == 1)
    def _():
        grad_over_first.wait_send()
        act_first.wait_send()
        for c in across_cores + late:
            c.wait_send()
        out_over.wait_send()

        @pl.when(off_diagonal)
        def _():
            out_late.wait_send()

    beside(handed, out_acts.at[1 - core], 0).wait_recv()
    beside(grad_second, out_grads.at[1 - core], 1).wait_recv()
    for c in vector_copies:
        c.wait_send()
    vec.wait_send()


def settle(*operands, collective_id):
    return comm_call(
        settle_kernel,
        [
            ((24, E), f32, VMEM), ((48, D), f32, VMEM), ((1, 24), f32, VMEM), ((K, 52), f32, VMEM), ((1, 52), f32, VMEM),
            ((1, 48), f32, VMEM), ((1, H), f32, VMEM), ((1, H), f32, VMEM), ((1, H), f32, VMEM), ((2, T, D), bf16, VMEM),
            ((2, T, D), f32, VMEM),
        ],
        [ANY] * 2 + [VMEM] * 12,
        [
            VMEM((96, EW), f32), VMEM((48, D), f32), VMEM((TP, 24, EW), f32),
            VMEM((2, 16, XW), f32), VMEM((3, 16, XW), f32), VMEM((7, 16, XW), f32), VMEM((TP, 16, XW), f32),
            VMEM((8, CONV + 128), f32), VMEM((8, CONV + 128), f32),
            *ring_halves(HALF, D), *ring_halves(HALF, D), VMEM((TP, HALO, D), bf16), VMEM((T, D), f32), VMEM((T, D), f32),
            VMEM((T, D), bf16),
            sems(2), sems(2), sems(2, 6), sems(2, 6), sems(10), sems(11), sems(3), sems(4), sems(4), sems(4), sems(2),
            sems(2), sems(1), sems(TP), sems(6, 6), sems(6, 6), sems(12), sems(12), sems(12),
            *sum_blocks(), *sum_blocks(), *ring_buffers(),
        ],
        collective_id,
        16 * 1024 * 1024,
    )(*operands)


def cut(array, offset, width):
    return lax.dynamic_slice_in_dim(array, offset, width, array.ndim - 1)


def cut_conv(array, place):
    return jnp.concatenate([cut(array, place * XW, XW), array[..., DI:CONV]], axis=-1)


def rms(values, gain):
    return values * row_scale(values) * gain


def layer_forward(normed, w_in, w_out, vecs, layer, collective_id):
    proj = jnp.dot(normed, w_in, preferred_element_type=f32)
    kept = forward_mix(proj, vecs, layer, collective_id)
    return jnp.dot(kept[0], w_out, preferred_element_type=f32), (normed, proj) + tuple(kept)


def layer_backward(gb, saved, w_in, w_out, vecs, layer, sums, collective_id):
    normed, proj, normed_two = saved[:3]
    gn = lax.dot_general(gb, w_out, (((1,), (1,)), ((), ())), preferred_element_type=f32)
    gp, partial, *more = backward_mix(gn, proj, saved[3:], vecs, w_in, layer, sums, collective_id)
    grad_out = lax.dot_general(normed_two, gb, (((0,), (0,)), ((), ())), preferred_element_type=f32).astype(bf16)
    grad_in = lax.dot_general(normed, gp, (((0,), (0,)), ((), ())), preferred_element_type=f32).astype(bf16)
    return partial, grad_in.reshape(4, 4, 96, EW), grad_out.reshape(4, 4, 48, D), more


def per_device(
    layer_input, output_grad, seq_lengths, norm_gain, in_proj, conv_weight, conv_bias, gate_gain, out_proj,
    decay_log, skip_gain, step_bias,
):
    core = lax.axis_index("section")
    x = lax.axis_index("x")
    y = lax.axis_index("y")
    z = lax.axis_index("z")
    positions = (y * 4 + x) * T + jnp.arange(T, dtype=jnp.int32)
    length = jnp.where(core == 0, seq_lengths[0, 0], seq_lengths[1, 0])
    valid = (positions < length).astype(f32)[:, None]
    entering = jnp.where(core == 0, layer_input[0, 0], layer_input[1, 0])
    given = (valid * jnp.where(core == 0, output_grad[0, 0], output_grad[1, 0]).astype(f32)).astype(bf16)
    own_in, own_out, w_in, w_out, vectors, heads, entering_all, given_all = collect(
        jnp.pad(in_proj[0], ((0, 0), (0, 2 * DI + 2 * N + 128 - E))),
        (out_proj[0], norm_gain, conv_weight[0], conv_bias, gate_gain, decay_log, skip_gain, step_bias),
        entering,
        given,
        0,
    )
    w_in = w_in.reshape(D, EW)
    w_out = w_out.reshape(XW, D)
    vectors = vectors.reshape(2, 64, 8, 128)
    gains = vectors[:, :, 0, :24].reshape(2, D)
    conv = vectors[:, :, 1:6, :52].transpose(0, 2, 1, 3).reshape(2, K + 1, CONV)
    gate = vectors[:, :, 6, :48].reshape(2, 1, DI)
    heads = cut(heads[:, 0:3, :H], x * HL, HL)

    def row(a):
        return jnp.pad(a, ((0, 0), (0, 0), (0, UW - a.shape[-1])))

    vecs = jnp.concatenate(
        [
            cut_conv(conv, x),
            row(cut(gate, x * XW, XW)),
            row(jnp.repeat(heads[:, 1:2], PS, axis=-1)),
            row(-jnp.exp(heads[:, 0:1])),
            row(heads[:, 2:3]),
            jnp.zeros((2, 7, UW), f32),
        ],
        axis=1,
    )

    normed = lax.optimization_barrier(rms(entering_all.astype(f32), gains[0]).astype(bf16))
    partial, saved_first = layer_forward(normed, w_in, w_out, vecs, 0, 1)
    handed, normed, late_w_in, late_w_out = relay_forward(partial, entering, valid, gains, own_in, own_out, 2)
    late_w_in = late_w_in.reshape(D, EW)
    late_w_out = late_w_out.reshape(XW, D)
    last_partial, saved_second = layer_forward(normed, late_w_in, late_w_out, vecs, 1, 3)
    partial, grad_in, grad_out, (vector_second,) = layer_backward(
        given_all, saved_second, late_w_in, late_w_out, vecs, 1, None, 4
    )
    grad_second, norm_second, back_all, *sums = relay_backward(partial, handed, valid, gains, given, grad_in, grad_out, 5)
    partial, grad_in, grad_out, (vector_first, late_in, late_out) = layer_backward(
        back_all, saved_first, w_in, w_out, vecs, 0, sums, 6
    )
    grad_in, grad_out, norm_g, conv_g, bias_g, gate_g, decay_g, skip_g, step_g, activations, input_grad = settle(
        grad_in,
        grad_out,
        vector_first,
        vector_second,
        norm_second,
        late_in,
        late_out,
        last_partial.astype(bf16),
        partial,
        entering,
        handed,
        valid,
        gains,
        grad_second,
        collective_id=7,
    )
    return (
        activations[None, :, None], input_grad[None, :, None], norm_g, grad_in[None], conv_g[None], bias_g, gate_g,
        grad_out[None], decay_g, skip_g, step_g,
    )


def solution(mesh):
    grid = jax.sharding.Mesh(mesh.devices.reshape(2, 4, 4, 4), ("section", "z", "y", "x"))
    rows = ("z", "y", "x")
    tokens = P(None, "z", ("y", "x"), None)
    both = P("section", None, "z", ("y", "x"), None)
    return jax.shard_map(
        per_device,
        mesh=grid,
        in_specs=(
            tokens,
            tokens,
            P(None, "z"),
            P("section", rows),
            P("section", rows, None),
            P("section", None, rows),
            P("section", rows),
            P("section", rows),
            P("section", rows, None),
            P("section", None),
            P("section", None),
            P("section", None),
        ),
        out_specs=(
            both,
            both,
            P("section", rows),
            P("section", rows, None),
            P("section", None, rows),
            P("section", rows),
            P("section", rows),
            P("section", rows, None),
            P("section", None),
            P("section", None),
            P("section", None),
        ),
        check_vma=False,
    )
```
